32 devices in a mesh: grp: 2 (over y), kin: 4 (over z), nout: 4 (over x, core).
Axes of the slice: x: 2, y: 2, z: 4, core: 2. Of those that a mesh axis runs over, the one named last changes fastest.
Arguments:
- normed: bfloat16 [64, 14848], P(('grp', 'nout'), 'kin'), parts along dimension 0, may hold values from -6 to 6
- keep_masks: int32 [16, 14848], P('grp', 'kin'), parts along dimension 0, may hold values 0 or 1
- qkv_weight: bfloat16 [14848, 15872], P('kin', 'nout'), may hold values from -0.046875 to 0.046875
- up_weight: bfloat16 [14848, 29696], P('kin', 'nout'), may hold values from -0.046875 to 0.046875
Outputs:
- qkv_out: bfloat16 [64, 8, 15872], P(('grp', 'kin'), None, 'nout'), parts along dimension 0
- hidden_out: bfloat16 [64, 8, 29696], P(('grp', 'kin'), None, 'nout'), parts along dimension 0
The draws below stay inside these ranges and needn't reach their ends.
There are 2 independent parts, one for each index of `grp`. The reference program is written for one: setup_inputs(seed, part) draws one part's arguments, and reference() takes and returns one part's arrays. A program takes and returns all parts, laid end to end along the dimension named above; an argument that names none is the same for every part. Nothing has to cross between parts.
All inputs are finite; a program needn't handle non-finite values. No bound on the sum of `keep_masks` on one device may be relied on, other than what follows from the above.
Results may differ from the reference program's by a relative error of at most 0.013.
Values may be sent and summed in bfloat16 or wider, within the bound.
A program may use at most 192 MiB of HBM per device.

```python
import jax
import jax.numpy as jnp
from jax import lax

D = 14848
QKV = 15872
FFW = 29696
PASSES = 8
TOKENS = 32
N_KIN = 4


def touch_ends(array, rng, least, high):
    extent = array.shape
    spot = [jax.random.randint(jax.random.fold_in(rng, axis), (), 0, extent[axis]) for axis in range(len(extent))]
    array = array.at[tuple(spot)].set(least)
    longest = extent.index(max(extent))
    spot[longest] = (spot[longest] + 1) % extent[longest]
    return array.at[tuple(spot)].set(high)


def levels(rng, shape, split, low, largest):
    gain = 1.0
    for position, shards_of in split:
        heights = jax.random.uniform(jax.random.fold_in(jax.random.fold_in(rng, 6), position), (shards_of,), jnp.float32, low / len(split), largest / len(split))
        gain = gain * jnp.repeat(jnp.exp(heights), shape[position] // shards_of).reshape((-1,) + (1,) * (len(shape) - 1 - position))
    return gain


def gaussian(rng, dims, deviation, limit, cuts=(), dtype=jnp.bfloat16):
    result = deviation * jax.random.normal(rng, dims, jnp.float32)
    if cuts:
        result = result * levels(rng, dims, cuts, -0.22, 0.18)
    return jnp.clip(result, -limit, limit).astype(dtype)


def setup_inputs(seed: int = 0, part: int = 0) -> dict:
    key_list = jax.random.split(jax.random.key(seed), 5)
    part_keys = jax.random.split(jax.random.fold_in(key_list[4], part), 5)
    normed = gaussian(part_keys[0], (TOKENS, D), 1.0, 6.0, ((0, 4), (1, 4)))
    keep_masks = touch_ends((jax.random.randint(part_keys[1], (PASSES, D), 0, 10) < 9).astype(jnp.int32), jax.random.fold_in(part_keys[1], 1), 0, 1)
    qkv_weight = gaussian(key_list[2], (D, QKV), D ** -0.5, 0.046875, ((0, 4), (1, 4)))
    up_weight = gaussian(key_list[3], (D, FFW), D ** -0.5, 0.046875, ((0, 4), (1, 4)))
    return dict(normed=normed, keep_masks=keep_masks, qkv_weight=qkv_weight, up_weight=up_weight)


KEEP_SCALE = 10.0 / 9.0


def block_summed(dropped, weight):
    width = dropped.shape[1] // N_KIN

    def add_block(index, total):
        start = (index * width).astype(jnp.int32)
        rows = lax.dynamic_slice_in_dim(dropped, start, width, 1)
        cols = lax.dynamic_slice_in_dim(weight, start, width, 0)
        piece = jnp.dot(rows, cols, preferred_element_type=jnp.float32).astype(jnp.bfloat16)
        piece = lax.optimization_barrier(piece)
        return total + piece.astype(jnp.float32)

    start_total = jnp.zeros((dropped.shape[0], weight.shape[1]), jnp.float32)
    return lax.fori_loop(0, N_KIN, add_block, start_total)


def reference(normed, keep_masks, qkv_weight, up_weight):
    dropped = normed.astype(jnp.float32)[:, None, :] * keep_masks.astype(jnp.float32)[None, :, :] * KEEP_SCALE
    dropped = dropped.astype(jnp.bfloat16).reshape(TOKENS * PASSES, D)
    qkv_sum = block_summed(dropped, qkv_weight)
    up_sum = block_summed(dropped, up_weight)
    qkv_out = qkv_sum.astype(jnp.bfloat16).reshape(TOKENS, PASSES, QKV)
    hidden_out = jax.nn.gelu(up_sum, approximate=False).astype(jnp.bfloat16).reshape(TOKENS, PASSES, FFW)
    return (qkv_out, hidden_out)
```

```python
import functools

import jax
import jax.numpy as jnp
from jax import lax
from jax.experimental import pallas as pl
from jax.experimental.pallas import tpu as pltpu
from jax.sharding import PartitionSpec as P

KEEP_SCALE = 10.0 / 9.0
WIDE = 256
SLOTS = 3
LAG = 3
MESH = pl.DeviceIdType.MESH


def gelu(v):
    return v * (1.0 + lax.erf(v * (0.5**0.5))) * 0.5


def kernel(
    n, peers, passes, head, nq, chunks,
    normed_ref, mask_ref, qkv_ref, up_ref, qkv_out, up_out,
    gathered, dropped, tiles, own, rising, falling,
    gather_send, gather_recv, tile_sem, send_sem, rise_recv, fall_recv,
):
    z = lax.axis_index("kin")
    mine = lax.axis_index("nout")
    above = jnp.minimum(z + 1, n - 1)
    below = jnp.maximum(z - 1, 0)
    block = own.shape[2]

    def tile_copy(c, slot):
        def go(act):
            @pl.when(c < nq)
            def _():
                col = pl.multiple_of(head + (c - 1) * WIDE, 128)
                act(pltpu.make_async_copy(qkv_ref.at[:, pl.ds(col, WIDE)], tiles.at[slot], tile_sem.at[slot]))

            @pl.when(c >= nq)
            def _():
                col = pl.multiple_of((c - nq) * WIDE, 128)
                act(pltpu.make_async_copy(up_ref.at[:, pl.ds(col, WIDE)], tiles.at[slot], tile_sem.at[slot]))
        return go

    first_tile = pltpu.make_async_copy(qkv_ref.at[:, pl.ds(0, head)], tiles.at[0, :, pl.ds(0, head)], tile_sem.at[0])
    first_tile.start()
    for c in range(1, min(SLOTS, chunks)):
        tile_copy(c, c)(lambda copy: copy.start())

    barrier = pltpu.get_barrier_semaphore()
    for k in range(1, peers):
        pl.semaphore_signal(barrier, inc=1, device_id={"nout": lax.rem(mine + k, peers)}, device_id_type=MESH)

    @pl.when(z < n - 1)
    def _():
        pl.semaphore_signal(barrier, inc=1, device_id={"kin": above}, device_id_type=MESH)

    @pl.when(z > 0)
    def _():
        pl.semaphore_signal(barrier, inc=1, device_id={"kin": below}, device_id_type=MESH)

    pl.semaphore_wait(barrier, peers - 1 + jnp.where(z < n - 1, 1, 0) + jnp.where(z > 0, 1, 0))

    def gather_copy(k):
        return pltpu.make_async_remote_copy(
            src_ref=normed_ref, dst_ref=gathered.at[k - 1],
            send_sem=gather_send.at[k - 1], recv_sem=gather_recv.at[k - 1],
            device_id={"nout": lax.rem(mine + k, peers)}, device_id_type=MESH,
        )

    for k in range(1, peers):
        gather_copy(k).start()

    keep = mask_ref[...].astype(jnp.float32)
    tokens = normed_ref.shape[0]

    def drop(x, source):
        x = x.astype(jnp.float32)
        for r in range(0, tokens, 2):
            pair = [x[t : t + 1, :] * keep * KEEP_SCALE for t in (r, r + 1)]
            row = pl.multiple_of((source * tokens + r) * passes, 2 * passes)
            dropped[pl.ds(row, 2 * passes), :] = jnp.concatenate(pair, axis=0).astype(jnp.bfloat16)

    drop(normed_ref[...], mine)
    for k in range(1, peers):
        gather_copy(k).wait_recv()
        drop(gathered[k - 1], lax.rem(mine - k + peers, peers))

    def sized(c, body):
        @pl.when(c == 0)
        def _():
            body(0, head)

        @pl.when((c > 0) & (c < chunks))
        def _():
            body(c, WIDE)

    def rise_copy(c, d, width):
        part = (c, d, slice(None), pl.ds(0, width))
        return pltpu.make_async_remote_copy(
            src_ref=rising.at[part], dst_ref=rising.at[part],
            send_sem=send_sem.at[c, d], recv_sem=rise_recv.at[c, d],
            device_id={"kin": above}, device_id_type=MESH,
        )

    def fall_copy(c, d, width):
        part = (c, d, slice(None), pl.ds(0, width))
        return pltpu.make_async_remote_copy(
            src_ref=falling.at[part], dst_ref=falling.at[part],
            send_sem=send_sem.at[c, d], recv_sem=fall_recv.at[c, d],
            device_id={"kin": below}, device_id_type=MESH,
        )

    def compute(c, width):
        slot = lax.rem(c, SLOTS)
        if width == WIDE and not isinstance(c, int):
            tile_copy(c, slot)(lambda copy: copy.wait())
        else:
            first_tile.wait()
        got = jnp.dot(dropped[...], tiles[slot, :, :width], preferred_element_type=jnp.float32)
        own[c, :, :, :width] = got.reshape(n, block, width)

        @pl.when(c + SLOTS < chunks)
        def _():
            tile_copy(c + SLOTS, slot)(lambda copy: copy.start())

    def forward(buffer, copy_of, at_end, count, target):
        def body(c, width):
            def one(i, carry):
                d = target(i)

                @pl.when(at_end)
                def _():
                    buffer[c, d, :, :width] = own[c, d, :, :width].astype(jnp.bfloat16)

                @pl.when(jnp.logical_not(at_end))
                def _():
                    copy_of(c, d, width).wait_recv()
                    buffer[c, d, :, :width] = (
                        buffer[c, d, :, :width].astype(jnp.float32) + own[c, d, :, :width]
                    ).astype(jnp.bfloat16)

                copy_of(c, d, width).start()
                return carry

            lax.fori_loop(0, count, one, 0)
        return body

    rise = forward(rising, rise_copy, z == 0, n - 1 - z, lambda i: n - 1 - i)
    fall = forward(falling, fall_copy, z == n - 1, z, lambda i: i)

    def finish(c, width):
        @pl.when(z > 0)
        def _():
            rise_copy(c, z, width).wait_recv()
            own[c, z, :, :width] += rising[c, z, :, :width].astype(jnp.float32)

        @pl.when(z < n - 1)
        def _():
            fall_copy(c, z, width).wait_recv()
            own[c, z, :, :width] += falling[c, z, :, :width].astype(jnp.float32)

        total = own[c, z, :, :width]
        if isinstance(c, int):
            qkv_out[:, :width] = total.astype(jnp.bfloat16)
        else:
            @pl.when(c < nq)
            def _():
                col = pl.multiple_of(head + (c - 1) * WIDE, 128)
                qkv_out[:, pl.ds(col, WIDE)] = total.astype(jnp.bfloat16)

            @pl.when(c >= nq)
            def _():
                col = pl.multiple_of((c - nq) * WIDE, 128)
                up_out[:, pl.ds(col, WIDE)] = gelu(total).astype(jnp.bfloat16)

    def step(s, carry):
        sized(s, compute)
        sized(s - LAG * z, rise)
        sized(s - LAG * (n - 1 - z), fall)
        sized(s - LAG * (n - 1), finish)
        return carry

    lax.fori_loop(0, chunks + LAG * (n - 1), step, 0)

    for k in range(1, peers):
        gather_copy(k).wait_send()

    def drain(c, width):
        def up(i, carry):
            rise_copy(c, n - 1 - i, width).wait_send()
            return carry

        def down(i, carry):
            fall_copy(c, i, width).wait_send()
            return carry

        lax.fori_loop(0, n - 1 - z, up, 0)
        lax.fori_loop(0, z, down, 0)

    def drain_step(c, carry):
        sized(c, drain)
        return carry

    lax.fori_loop(0, chunks, drain_step, 0)


def fused(normed, keep_masks, qkv_weight, up_weight):
    n, peers = lax.axis_size("kin"), lax.axis_size("nout")
    tokens, width = normed.shape
    passes = keep_masks.shape[0]
    qkv_cols, up_cols = qkv_weight.shape[1], up_weight.shape[1]
    head = qkv_cols % WIDE or WIDE
    nq = 1 + (qkv_cols - head) // WIDE
    chunks = nq + up_cols // WIDE
    rows = tokens * peers * passes
    block = rows // n
    vmem = pl.BlockSpec(memory_space=pltpu.VMEM)
    hbm = pl.BlockSpec(memory_space=pl.ANY)
    qkv_out, up_out = pl.pallas_call(
        functools.partial(kernel, n, peers, passes, head, nq, chunks),
        out_shape=(
            jax.ShapeDtypeStruct((block, qkv_cols), jnp.bfloat16),
            jax.ShapeDtypeStruct((block, up_cols), jnp.bfloat16),
        ),
        in_specs=[vmem, vmem, hbm, hbm],
        out_specs=(vmem, vmem),
        scratch_shapes=[
            pltpu.VMEM((peers - 1, tokens, width), jnp.bfloat16),
            pltpu.VMEM((rows, width), jnp.bfloat16),
            pltpu.VMEM((SLOTS, width, WIDE), jnp.bfloat16),
            pltpu.VMEM((chunks, n, block, WIDE), jnp.float32),
            pltpu.VMEM((chunks, n, block, WIDE), jnp.bfloat16),
            pltpu.VMEM((chunks, n, block, WIDE), jnp.bfloat16),
            pltpu.SemaphoreType.DMA((peers - 1,)),
            pltpu.SemaphoreType.DMA((peers - 1,)),
            pltpu.SemaphoreType.DMA((SLOTS,)),
            pltpu.SemaphoreType.DMA((chunks, n)),
            pltpu.SemaphoreType.DMA((chunks, n)),
            pltpu.SemaphoreType.DMA((chunks, n)),
        ],
        compiler_params=pltpu.CompilerParams(
            collective_id=0, has_side_effects=True, vmem_limit_bytes=52 * 2**20
        ),
        cost_estimate=pl.CostEstimate(
            flops=2 * rows * width * (qkv_cols + up_cols),
            bytes_accessed=2 * width * (qkv_cols + up_cols),
            transcendentals=block * up_cols,
        ),
    )(normed, keep_masks, qkv_weight, up_weight)
    own_tokens = block // passes
    return (
        qkv_out.reshape(own_tokens, passes, qkv_cols),
        up_out.reshape(own_tokens, passes, up_cols),
    )


def plain(normed, keep_masks, qkv_weight, up_weight):
    gathered = lax.all_gather(normed, "nout", axis=0, tiled=True)
    all_tokens, width = gathered.shape
    passes = keep_masks.shape[0]
    qkv_cols, up_cols = qkv_weight.shape[1], up_weight.shape[1]
    dropped = (
        gathered.astype(jnp.float32)[:, None, :]
        * keep_masks.astype(jnp.float32)[None, :, :]
        * KEEP_SCALE
    )
    rows = dropped.astype(jnp.bfloat16).reshape(all_tokens * passes, width)
    first = jnp.dot(rows, qkv_weight, preferred_element_type=jnp.float32)
    second = jnp.dot(rows, up_weight, preferred_element_type=jnp.float32)
    joined = jnp.concatenate([first, second], axis=1)
    summed = lax.psum_scatter(
        joined.reshape(all_tokens, passes, qkv_cols + up_cols).astype(jnp.bfloat16),
        "kin",
        scatter_dimension=0,
        tiled=True,
    ).astype(jnp.float32)
    qkv_out = summed[:, :, :qkv_cols].astype(jnp.bfloat16)
    hidden_out = jax.nn.gelu(summed[:, :, qkv_cols:], approximate=False).astype(jnp.bfloat16)
    return (qkv_out, hidden_out)


def local(normed, keep_masks, qkv_weight, up_weight):
    tokens, width = normed.shape
    passes = keep_masks.shape[0]
    n, peers = lax.axis_size("kin"), lax.axis_size("nout")
    aligned = (
        width % 128 == 0
        and qkv_weight.shape[1] % 128 == 0
        and up_weight.shape[1] % WIDE == 0
        and tokens % 2 == 0
        and passes == 8
        and (tokens * peers * passes // n) % 16 == 0
    )
    run = fused if aligned else plain
    return run(normed, keep_masks, qkv_weight, up_weight)


def solution(mesh):
    placed = (P(("grp", "nout"), "kin"), P("grp", "kin"), P("kin", "nout"), P("kin", "nout"))
    return jax.shard_map(
        local,
        mesh=mesh,
        in_specs=placed,
        out_specs=(P(("grp", "kin"), None, "nout"), P(("grp", "kin"), None, "nout")),
        check_vma=False,
    )
```

```python
import functools

import jax
import jax.numpy as jnp
from jax import lax
from jax.experimental import pallas as pl
from jax.experimental.pallas import tpu as pltpu
from jax.sharding import PartitionSpec as P

KEEP_SCALE = 10.0 / 9.0
WIDE = 256
SLOTS = 3
LAG = 4
MESH = pl.DeviceIdType.MESH


def gelu(v):
    return v * (1.0 + lax.erf(v * (0.5**0.5))) * 0.5


def kernel(
    n, peers, passes, head, nq, chunks,
    normed_ref, mask_ref, qkv_ref, up_ref, qkv_out, up_out,
    gathered, mask, dropped, tiles, own, rising, falling,
    own_sem, mask_sem, gather_send, gather_recv, tile_sem, send_sem, rise_recv, fall_recv,
):
    z = lax.axis_index("kin")
    mine = lax.axis_index("nout")
    above = jnp.minimum(z + 1, n - 1)
    below = jnp.maximum(z - 1, 0)
    block = own.shape[2]

    def tile_copy(c, slot):
        def go(act):
            @pl.when(c < nq)
            def _():
                col = pl.multiple_of(head + (c - 1) * WIDE, 128)
                act(pltpu.make_async_copy(qkv_ref.at[:, pl.ds(col, WIDE)], tiles.at[slot], tile_sem.at[slot]))

            @pl.when(c >= nq)
            def _():
                col = pl.multiple_of((c - nq) * WIDE, 128)
                act(pltpu.make_async_copy(up_ref.at[:, pl.ds(col, WIDE)], tiles.at[slot], tile_sem.at[slot]))
        return go

    own_copy = pltpu.make_async_copy(normed_ref, gathered.at[0], own_sem)
    own_copy.start()
    mask_copy = pltpu.make_async_copy(mask_ref, mask, mask_sem)
    mask_copy.start()
    first_tile = pltpu.make_async_copy(qkv_ref.at[:, pl.ds(0, head)], tiles.at[0, :, pl.ds(0, head)], tile_sem.at[0])
    first_tile.start()
    def peer(k):
        at = mine
        bit = 1
        while bit < peers:
            if k & bit:
                at = at + bit - 2 * bit * ((mine // bit) % 2)
            bit *= 2
        return at

    barrier = pltpu.get_barrier_semaphore()
    for k in range(1, peers):
        pl.semaphore_signal(barrier, inc=1, device_id={"nout": peer(k)}, device_id_type=MESH)

    @pl.when(z < n - 1)
    def _():
        pl.semaphore_signal(barrier, inc=1, device_id={"kin": above}, device_id_type=MESH)

    @pl.when(z > 0)
    def _():
        pl.semaphore_signal(barrier, inc=1, device_id={"kin": below}, device_id_type=MESH)

    pl.semaphore_wait(barrier, peers - 1 + jnp.where(z < n - 1, 1, 0) + jnp.where(z > 0, 1, 0))

    def gather_copy(k):
        return pltpu.make_async_remote_copy(
            src_ref=normed_ref, dst_ref=gathered.at[k],
            send_sem=gather_send.at[k - 1], recv_sem=gather_recv.at[k - 1],
            device_id={"nout": peer(k)}, device_id_type=MESH,
        )

    for k in range(peers - 1, 0, -1):
        gather_copy(k).start()
    for c in range(1, min(SLOTS, chunks)):
        tile_copy(c, c)(lambda copy: copy.start())

    mask_copy.wait()
    keep = mask[...].astype(jnp.float32)
    tokens = normed_ref.shape[0]

    def drop(x, source):
        x = x.astype(jnp.float32)
        for r in range(0, tokens, 2):
            pair = [x[t : t + 1, :] * keep * KEEP_SCALE for t in (r, r + 1)]
            row = pl.multiple_of((source * tokens + r) * passes, 2 * passes)
            dropped[pl.ds(row, 2 * passes), :] = jnp.concatenate(pair, axis=0).astype(jnp.bfloat16)

    own_copy.wait()
    drop(gathered[0], mine)
    for k in range(1, peers):
        gather_copy(k).wait_recv()
        drop(gathered[k], peer(k))

    def sized(c, body):
        @pl.when(c == 0)
        def _():
            body(0, head)

        @pl.when((c > 0) & (c < chunks))
        def _():
            body(c, WIDE)

    def rise_copy(c, d, width):
        part = (c, d, slice(None), pl.ds(0, width))
        return pltpu.make_async_remote_copy(
            src_ref=rising.at[part], dst_ref=rising.at[part],
            send_sem=send_sem.at[c, d], recv_sem=rise_recv.at[c, d],
            device_id={"kin": above}, device_id_type=MESH,
        )

    def fall_copy(c, d, width):
        part = (c, d, slice(None), pl.ds(0, width))
        return pltpu.make_async_remote_copy(
            src_ref=falling.at[part], dst_ref=falling.at[part],
            send_sem=send_sem.at[c, d], recv_sem=fall_recv.at[c, d],
            device_id={"kin": below}, device_id_type=MESH,
        )

    def compute(c, width):
        slot = lax.rem(c, SLOTS)
        if width == WIDE and not isinstance(c, int):
            tile_copy(c, slot)(lambda copy: copy.wait())
        else:
            first_tile.wait()
        got = jnp.dot(dropped[...], tiles[slot, :, :width], preferred_element_type=jnp.float32)
        own[c, :, :, :width] = got.reshape(n, block, width)

        @pl.when(c + SLOTS < chunks)
        def _():
            tile_copy(c + SLOTS, slot)(lambda copy: copy.start())

    def forward(buffer, copy_of, at_end, d):
        def body(c, width):
            @pl.when(at_end)
            def _():
                buffer[c, d, :, :width] = own[c, d, :, :width].astype(jnp.bfloat16)

            @pl.when(jnp.logical_not(at_end))
            def _():
                copy_of(c, d, width).wait_recv()
                buffer[c, d, :, :width] = (
                    buffer[c, d, :, :width].astype(jnp.float32) + own[c, d, :, :width]
                ).astype(jnp.bfloat16)

            copy_of(c, d, width).start()
        return body

    def finish(c, width):
        @pl.when(z > 0)
        def _():
            rise_copy(c, z, width).wait_recv()
            own[c, z, :, :width] += rising[c, z, :, :width].astype(jnp.float32)

        @pl.when(z < n - 1)
        def _():
            fall_copy(c, z, width).wait_recv()
            own[c, z, :, :width] += falling[c, z, :, :width].astype(jnp.float32)

        total = own[c, z, :, :width]
        if isinstance(c, int):
            qkv_out[:, :width] = total.astype(jnp.bfloat16)
        else:
            @pl.when(c < nq)
            def _():
                col = pl.multiple_of(head + (c - 1) * WIDE, 128)
                qkv_out[:, pl.ds(col, WIDE)] = total.astype(jnp.bfloat16)

            @pl.when(c >= nq)
            def _():
                col = pl.multiple_of((c - nq) * WIDE, 128)
                up_out[:, pl.ds(col, WIDE)] = gelu(total).astype(jnp.bfloat16)

    def step(s, carry):
        sized(s, compute)

        def rise(i, carry):
            d = n - 1 - i
            sized(s - LAG * (z + i), forward(rising, rise_copy, z == 0, d))
            return carry

        def fall(d, carry):
            sized(s - LAG * (n - 1 - z + d), forward(falling, fall_copy, z == n - 1, d))
            return carry

        lax.fori_loop(0, n - 1 - z, rise, 0)
        lax.fori_loop(0, z, fall, 0)
        sized(s - LAG * (n - 1), finish)
        return carry

    lax.fori_loop(0, chunks + LAG * (n - 1), step, 0)

    for k in range(1, peers):
        gather_copy(k).wait_send()

    def drain(c, width):
        def up(i, carry):
            rise_copy(c, n - 1 - i, width).wait_send()
            return carry

        def down(i, carry):
            fall_copy(c, i, width).wait_send()
            return carry

        lax.fori_loop(0, n - 1 - z, up, 0)
        lax.fori_loop(0, z, down, 0)

    def drain_step(c, carry):
        sized(c, drain)
        return carry

    lax.fori_loop(0, chunks, drain_step, 0)


def fused(normed, keep_masks, qkv_weight, up_weight):
    n, peers = lax.axis_size("kin"), lax.axis_size("nout")
    tokens, width = normed.shape
    passes = keep_masks.shape[0]
    qkv_cols, up_cols = qkv_weight.shape[1], up_weight.shape[1]
    head = qkv_cols % WIDE or WIDE
    nq = 1 + (qkv_cols - head) // WIDE
    chunks = nq + up_cols // WIDE
    rows = tokens * peers * passes
    block = rows // n
    vmem = pl.BlockSpec(memory_space=pltpu.VMEM)
    hbm = pl.BlockSpec(memory_space=pl.ANY)
    qkv_out, up_out = pl.pallas_call(
        functools.partial(kernel, n, peers, passes, head, nq, chunks),
        out_shape=(
            jax.ShapeDtypeStruct((block, qkv_cols), jnp.bfloat16),
            jax.ShapeDtypeStruct((block, up_cols), jnp.bfloat16),
        ),
        in_specs=[hbm, hbm, hbm, hbm],
        out_specs=(vmem, vmem),
        scratch_shapes=[
            pltpu.VMEM((peers, tokens, width), jnp.bfloat16),
            pltpu.VMEM((passes, width), jnp.int32),
            pltpu.VMEM((rows, width), jnp.bfloat16),
            pltpu.VMEM((SLOTS, width, WIDE), jnp.bfloat16),
            pltpu.VMEM((chunks, n, block, WIDE), jnp.float32),
            pltpu.VMEM((chunks, n, block, WIDE), jnp.bfloat16),
            pltpu.VMEM((chunks, n, block, WIDE), jnp.bfloat16),
            pltpu.SemaphoreType.DMA,
            pltpu.SemaphoreType.DMA,
            pltpu.SemaphoreType.DMA((peers - 1,)),
            pltpu.SemaphoreType.DMA((peers - 1,)),
            pltpu.SemaphoreType.DMA((SLOTS,)),
            pltpu.SemaphoreType.DMA((chunks, n)),
            pltpu.SemaphoreType.DMA((chunks, n)),
            pltpu.SemaphoreType.DMA((chunks, n)),
        ],
        compiler_params=pltpu.CompilerParams(
            collective_id=0, has_side_effects=True, vmem_limit_bytes=52 * 2**20
        ),
        cost_estimate=pl.CostEstimate(
            flops=2 * rows * width * (qkv_cols + up_cols),
            bytes_accessed=2 * width * (qkv_cols + up_cols),
            transcendentals=block * up_cols,
        ),
    )(normed, keep_masks, qkv_weight, up_weight)
    own_tokens = block // passes
    return (
        qkv_out.reshape(own_tokens, passes, qkv_cols),
        up_out.reshape(own_tokens, passes, up_cols),
    )


def plain(normed, keep_masks, qkv_weight, up_weight):
    gathered = lax.all_gather(normed, "nout", axis=0, tiled=True)
    all_tokens, width = gathered.shape
    passes = keep_masks.shape[0]
    qkv_cols, up_cols = qkv_weight.shape[1], up_weight.shape[1]
    dropped = (
        gathered.astype(jnp.float32)[:, None, :]
        * keep_masks.astype(jnp.float32)[None, :, :]
        * KEEP_SCALE
    )
    rows = dropped.astype(jnp.bfloat16).reshape(all_tokens * passes, width)
    first = jnp.dot(rows, qkv_weight, preferred_element_type=jnp.float32)
    second = jnp.dot(rows, up_weight, preferred_element_type=jnp.float32)
    joined = jnp.concatenate([first, second], axis=1)
    summed = lax.psum_scatter(
        joined.reshape(all_tokens, passes, qkv_cols + up_cols).astype(jnp.bfloat16),
        "kin",
        scatter_dimension=0,
        tiled=True,
    ).astype(jnp.float32)
    qkv_out = summed[:, :, :qkv_cols].astype(jnp.bfloat16)
    hidden_out = jax.nn.gelu(summed[:, :, qkv_cols:], approximate=False).astype(jnp.bfloat16)
    return (qkv_out, hidden_out)


def local(normed, keep_masks, qkv_weight, up_weight):
    tokens, width = normed.shape
    passes = keep_masks.shape[0]
    n, peers = lax.axis_size("kin"), lax.axis_size("nout")
    aligned = (
        width % 128 == 0
        and qkv_weight.shape[1] % 128 == 0
        and up_weight.shape[1] % WIDE == 0
        and tokens % 2 == 0
        and peers & (peers - 1) == 0
        and passes == 8
        and (tokens * peers * passes // n) % 16 == 0
    )
    run = fused if aligned else plain
    return run(normed, keep_masks, qkv_weight, up_weight)


def solution(mesh):
    placed = (P(("grp", "nout"), "kin"), P("grp", "kin"), P("kin", "nout"), P("kin", "nout"))
    return jax.shard_map(
        local,
        mesh=mesh,
        in_specs=placed,
        out_specs=(P(("grp", "kin"), None, "nout"), P(("grp", "kin"), None, "nout")),
        check_vma=False,
    )
```

```python
import functools

import jax
import jax.numpy as jnp
from jax import lax
from jax.experimental import pallas as pl
from jax.experimental.pallas import tpu as pltpu
from jax.sharding import PartitionSpec as P

KEEP_SCALE = 10.0 / 9.0
WIDE = 256
SLOTS = 8
EARLY = 6
LAG = 4
MESH = pl.DeviceIdType.MESH


def gelu(v):
    return v * (1.0 + lax.erf(v * (0.5**0.5))) * 0.5


def kernel(
    n, peers, passes, head, nq, chunks,
    normed_ref, mask_ref, qkv_ref, up_ref, qkv_out, up_out,
    gathered, mask, dropped, tiles, own, rising, falling,
    own_sem, mask_sem, gather_send, gather_recv, tile_sem, send_sem, rise_recv, fall_recv,
):
    z = lax.axis_index("kin")
    mine = lax.axis_index("nout")
    above = jnp.minimum(z + 1, n - 1)
    below = jnp.maximum(z - 1, 0)
    block = own.shape[2]

    def tile_copy(c, slot):
        def go(act):
            @pl.when(c < nq)
            def _():
                col = pl.multiple_of(head + (c - 1) * WIDE, 128)
                act(pltpu.make_async_copy(qkv_ref.at[:, pl.ds(col, WIDE)], tiles.at[slot], tile_sem.at[slot]))

            @pl.when(c >= nq)
            def _():
                col = pl.multiple_of((c - nq) * WIDE, 128)
                act(pltpu.make_async_copy(up_ref.at[:, pl.ds(col, WIDE)], tiles.at[slot], tile_sem.at[slot]))
        return go

    own_copy = pltpu.make_async_copy(normed_ref, gathered.at[0], own_sem)
    own_copy.start()
    mask_copy = pltpu.make_async_copy(mask_ref, mask, mask_sem)
    mask_copy.start()
    first_tile = pltpu.make_async_copy(qkv_ref.at[:, pl.ds(0, head)], tiles.at[0, :, pl.ds(0, head)], tile_sem.at[0])
    first_tile.start()
    for c in range(1, min(SLOTS, chunks)):
        tile_copy(c, c)(lambda copy: copy.start())

    def peer(k):
        at = mine
        bit = 1
        while bit < peers:
            if k & bit:
                at = at + bit - 2 * bit * ((mine // bit) % 2)
            bit *= 2
        return at

    barrier = pltpu.get_barrier_semaphore()
    for k in range(1, peers):
        pl.semaphore_signal(barrier, inc=1, device_id={"nout": peer(k)}, device_id_type=MESH)

    @pl.when(z < n - 1)
    def _():
        pl.semaphore_signal(barrier, inc=1, device_id={"kin": above}, device_id_type=MESH)

    @pl.when(z > 0)
    def _():
        pl.semaphore_signal(barrier, inc=1, device_id={"kin": below}, device_id_type=MESH)

    own_copy.wait()
    pl.semaphore_wait(barrier, peers - 1 + jnp.where(z < n - 1, 1, 0) + jnp.where(z > 0, 1, 0))

    def gather_copy(k):
        return pltpu.make_async_remote_copy(
            src_ref=gathered.at[0], dst_ref=gathered.at[k],
            send_sem=gather_send.at[k - 1], recv_sem=gather_recv.at[k - 1],
            device_id={"nout": peer(k)}, device_id_type=MESH,
        )

    for k in range(peers - 1, 0, -1):
        gather_copy(k).start()
    mask_copy.wait()
    keep = mask[...].astype(jnp.float32) * KEEP_SCALE
    tokens = normed_ref.shape[0]

    def drop(x, source):
        x = x.astype(jnp.float32)
        for r in range(0, tokens, 2):
            pair = [x[t : t + 1, :] * keep for t in (r, r + 1)]
            row = pl.multiple_of((source * tokens + r) * passes, 2 * passes)
            dropped[pl.ds(row, 2 * passes), :] = jnp.concatenate(pair, axis=0).astype(jnp.bfloat16)

    drop(gathered[0], mine)

    def sized(c, body):
        @pl.when(c == 0)
        def _():
            body(0, head)

        @pl.when((c > 0) & (c < chunks))
        def _():
            body(c, WIDE)

    def rise_copy(c, d, width):
        part = (c, d, slice(None), pl.ds(0, width))
        return pltpu.make_async_remote_copy(
            src_ref=rising.at[part], dst_ref=rising.at[part],
            send_sem=send_sem.at[c, d], recv_sem=rise_recv.at[c, d],
            device_id={"kin": above}, device_id_type=MESH,
        )

    def fall_copy(c, d, width):
        part = (c, d, slice(None), pl.ds(0, width))
        return pltpu.make_async_remote_copy(
            src_ref=falling.at[part], dst_ref=falling.at[part],
            send_sem=send_sem.at[c, d], recv_sem=fall_recv.at[c, d],
            device_id={"kin": below}, device_id_type=MESH,
        )

    def compute(c, width):
        slot = lax.rem(c, SLOTS)
        if not isinstance(c, int):
            @pl.when(c >= EARLY)
            def _():
                tile_copy(c, slot)(lambda copy: copy.wait())

        got = jnp.dot(dropped[...], tiles[slot, :, :width], preferred_element_type=jnp.float32)
        own[c, :, :, :width] = got.reshape(n, block, width)

        @pl.when(c + SLOTS < chunks)
        def _():
            tile_copy(c + SLOTS, slot)(lambda copy: copy.start())

    for c in range(EARLY):
        width = WIDE if c else head
        if c:
            tile_copy(c, c)(lambda copy: copy.wait())
        else:
            first_tile.wait()

        def send_early(buffer, copy_of):
            rows = dropped[pl.ds(pl.multiple_of(mine * block, block), block), :]
            part = jnp.dot(rows, tiles[c, :, :width], preferred_element_type=jnp.float32)
            buffer[c, mine, :, :width] = part.astype(jnp.bfloat16)
            copy_of(c, mine, width).start()

        @pl.when((z == 0) & (mine > 0))
        def _():
            send_early(rising, rise_copy)

        @pl.when((z == n - 1) & (mine < n - 1))
        def _():
            send_early(falling, fall_copy)

    for k in range(1, peers):
        gather_copy(k).wait_recv()
        drop(gathered[k], peer(k))

    def forward(buffer, copy_of, at_end, d):
        def body(c, width):
            sent = at_end & (d == mine) & (c < EARLY)

            @pl.when(at_end & jnp.logical_not(sent))
            def _():
                buffer[c, d, :, :width] = own[c, d, :, :width].astype(jnp.bfloat16)

            @pl.when(jnp.logical_not(at_end))
            def _():
                copy_of(c, d, width).wait_recv()
                buffer[c, d, :, :width] = (
                    buffer[c, d, :, :width].astype(jnp.float32) + own[c, d, :, :width]
                ).astype(jnp.bfloat16)

            @pl.when(jnp.logical_not(sent))
            def _():
                copy_of(c, d, width).start()
        return body

    def finish(c, width):
        @pl.when(z > 0)
        def _():
            rise_copy(c, z, width).wait_recv()
            own[c, z, :, :width] += rising[c, z, :, :width].astype(jnp.float32)

        @pl.when(z < n - 1)
        def _():
            fall_copy(c, z, width).wait_recv()
            own[c, z, :, :width] += falling[c, z, :, :width].astype(jnp.float32)

        total = own[c, z, :, :width]
        if isinstance(c, int):
            qkv_out[:, :width] = total.astype(jnp.bfloat16)
        else:
            @pl.when(c < nq)
            def _():
                col = pl.multiple_of(head + (c - 1) * WIDE, 128)
                qkv_out[:, pl.ds(col, WIDE)] = total.astype(jnp.bfloat16)

            @pl.when(c >= nq)
            def _():
                col = pl.multiple_of((c - nq) * WIDE, 128)
                up_out[:, pl.ds(col, WIDE)] = gelu(total).astype(jnp.bfloat16)

    def step(s, carry):
        sized(s, compute)

        def rise(i, carry):
            d = n - 1 - i
            sized(s - LAG * (z + i), forward(rising, rise_copy, z == 0, d))
            return carry

        def fall(d, carry):
            sized(s - LAG * (n - 1 - z + d), forward(falling, fall_copy, z == n - 1, d))
            return carry

        lax.fori_loop(0, n - 1 - z, rise, 0)
        lax.fori_loop(0, z, fall, 0)
        sized(s - LAG * (n - 1), finish)
        return carry

    lax.fori_loop(0, chunks + LAG * (n - 1), step, 0)

    for k in range(1, peers):
        gather_copy(k).wait_send()

    def drain(c, width):
        def up(i, carry):
            rise_copy(c, n - 1 - i, width).wait_send()
            return carry

        def down(i, carry):
            fall_copy(c, i, width).wait_send()
            return carry

        lax.fori_loop(0, n - 1 - z, up, 0)
        lax.fori_loop(0, z, down, 0)

    def drain_step(c, carry):
        sized(c, drain)
        return carry

    lax.fori_loop(0, chunks, drain_step, 0)


def fused(normed, keep_masks, qkv_weight, up_weight):
    n, peers = lax.axis_size("kin"), lax.axis_size("nout")
    tokens, width = normed.shape
    passes = keep_masks.shape[0]
    qkv_cols, up_cols = qkv_weight.shape[1], up_weight.shape[1]
    head = qkv_cols % WIDE or WIDE
    nq = 1 + (qkv_cols - head) // WIDE
    chunks = nq + up_cols // WIDE
    rows = tokens * peers * passes
    block = rows // n
    vmem = pl.BlockSpec(memory_space=pltpu.VMEM)
    hbm = pl.BlockSpec(memory_space=pltpu.HBM)
    qkv_out, up_out = pl.pallas_call(
        functools.partial(kernel, n, peers, passes, head, nq, chunks),
        out_shape=(
            jax.ShapeDtypeStruct((block, qkv_cols), jnp.bfloat16),
            jax.ShapeDtypeStruct((block, up_cols), jnp.bfloat16),
        ),
        in_specs=[hbm, hbm, hbm, hbm],
        out_specs=(vmem, vmem),
        scratch_shapes=[
            pltpu.VMEM((peers, tokens, width), jnp.bfloat16),
            pltpu.VMEM((passes, width), jnp.int32),
            pltpu.VMEM((rows, width), jnp.bfloat16),
            pltpu.VMEM((SLOTS, width, WIDE), jnp.bfloat16),
            pltpu.VMEM((chunks, n, block, WIDE), jnp.float32),
            pltpu.VMEM((chunks, n, block, WIDE), jnp.bfloat16),
            pltpu.VMEM((chunks, n, block, WIDE), jnp.bfloat16),
            pltpu.SemaphoreType.DMA,
            pltpu.SemaphoreType.DMA,
            pltpu.SemaphoreType.DMA((peers - 1,)),
            pltpu.SemaphoreType.DMA((peers - 1,)),
            pltpu.SemaphoreType.DMA((SLOTS,)),
            pltpu.SemaphoreType.DMA((chunks, n)),
            pltpu.SemaphoreType.DMA((chunks, n)),
            pltpu.SemaphoreType.DMA((chunks, n)),
        ],
        compiler_params=pltpu.CompilerParams(
            collective_id=0, has_side_effects=True, vmem_limit_bytes=52 * 2**20
        ),
        cost_estimate=pl.CostEstimate(
            flops=2 * rows * width * (qkv_cols + up_cols),
            bytes_accessed=2 * width * (qkv_cols + up_cols),
            transcendentals=block * up_cols,
        ),
    )(normed, keep_masks, qkv_weight, up_weight)
    own_tokens = block // passes
    return (
        qkv_out.reshape(own_tokens, passes, qkv_cols),
        up_out.reshape(own_tokens, passes, up_cols),
    )


def plain(normed, keep_masks, qkv_weight, up_weight):
    gathered = lax.all_gather(normed, "nout", axis=0, tiled=True)
    all_tokens, width = gathered.shape
    passes = keep_masks.shape[0]
    qkv_cols, up_cols = qkv_weight.shape[1], up_weight.shape[1]
    dropped = (
        gathered.astype(jnp.float32)[:, None, :]
        * keep_masks.astype(jnp.float32)[None, :, :]
        * KEEP_SCALE
    )
    rows = dropped.astype(jnp.bfloat16).reshape(all_tokens * passes, width)
    first = jnp.dot(rows, qkv_weight, preferred_element_type=jnp.float32)
    second = jnp.dot(rows, up_weight, preferred_element_type=jnp.float32)
    joined = jnp.concatenate([first, second], axis=1)
    summed = lax.psum_scatter(
        joined.reshape(all_tokens, passes, qkv_cols + up_cols).astype(jnp.bfloat16),
        "kin",
        scatter_dimension=0,
        tiled=True,
    ).astype(jnp.float32)
    qkv_out = summed[:, :, :qkv_cols].astype(jnp.bfloat16)
    hidden_out = jax.nn.gelu(summed[:, :, qkv_cols:], approximate=False).astype(jnp.bfloat16)
    return (qkv_out, hidden_out)


def local(normed, keep_masks, qkv_weight, up_weight):
    tokens, width = normed.shape
    passes = keep_masks.shape[0]
    n, peers = lax.axis_size("kin"), lax.axis_size("nout")
    aligned = (
        width % 128 == 0
        and qkv_weight.shape[1] % 128 == 0
        and up_weight.shape[1] % WIDE == 0
        and tokens % 2 == 0
        and peers & (peers - 1) == 0
        and peers == n
        and passes == 8
        and (tokens * peers * passes // n) % 16 == 0
        and (qkv_weight.shape[1] + up_weight.shape[1]) // WIDE >= SLOTS
    )
    run = fused if aligned else plain
    return run(normed, keep_masks, qkv_weight, up_weight)


def solution(mesh):
    placed = (P(("grp", "nout"), "kin"), P("grp", "kin"), P("kin", "nout"), P("kin", "nout"))
    return jax.shard_map(
        local,
        mesh=mesh,
        in_specs=placed,
        out_specs=(P(("grp", "kin"), None, "nout"), P(("grp", "kin"), None, "nout")),
        check_vma=False,
    )
```

```python
import functools

import jax
import jax.numpy as jnp
from jax import lax
from jax.experimental import pallas as pl
from jax.experimental.pallas import tpu as pltpu
from jax.sharding import PartitionSpec as P

KEEP_SCALE = 10.0 / 9.0
WIDE = 256
SLOTS = 8
EARLY = 6
LAG = 3
MESH = pl.DeviceIdType.MESH


def gelu(v):
    return v * (1.0 + lax.erf(v * (0.5**0.5))) * 0.5


def kernel(
    n, peers, passes, head, nq, chunks,
    normed_ref, mask_ref, qkv_ref, up_ref, qkv_out, up_out,
    gathered, mask, dropped, tiles, own, rising, falling,
    own_sem, mask_sem, gather_send, gather_recv, tile_sem, send_sem, rise_recv, fall_recv,
):
    z = lax.axis_index("kin")
    mine = lax.axis_index("nout")
    above = jnp.minimum(z + 1, n - 1)
    below = jnp.maximum(z - 1, 0)
    block = own.shape[2]

    def tile_copy(c, slot):
        def go(act):
            @pl.when(c < nq)
            def _():
                col = pl.multiple_of(head + (c - 1) * WIDE, 128)
                act(pltpu.make_async_copy(qkv_ref.at[:, pl.ds(col, WIDE)], tiles.at[slot], tile_sem.at[slot]))

            @pl.when(c >= nq)
            def _():
                col = pl.multiple_of((c - nq) * WIDE, 128)
                act(pltpu.make_async_copy(up_ref.at[:, pl.ds(col, WIDE)], tiles.at[slot], tile_sem.at[slot]))
        return go

    own_copy = pltpu.make_async_copy(normed_ref, gathered.at[0], own_sem)
    own_copy.start()
    mask_copy = pltpu.make_async_copy(mask_ref, mask, mask_sem)
    mask_copy.start()
    first_tile = pltpu.make_async_copy(qkv_ref.at[:, pl.ds(0, head)], tiles.at[0, :, pl.ds(0, head)], tile_sem.at[0])
    first_tile.start()
    for c in range(1, min(SLOTS, chunks)):
        tile_copy(c, c)(lambda copy: copy.start())

    def peer(k):
        at = mine
        bit = 1
        while bit < peers:
            if k & bit:
                at = at + bit - 2 * bit * ((mine // bit) % 2)
            bit *= 2
        return at

    barrier = pltpu.get_barrier_semaphore()
    for k in range(1, peers):
        pl.semaphore_signal(barrier, inc=1, device_id={"nout": peer(k)}, device_id_type=MESH)

    @pl.when(z < n - 1)
    def _():
        pl.semaphore_signal(barrier, inc=1, device_id={"kin": above}, device_id_type=MESH)

    @pl.when(z > 0)
    def _():
        pl.semaphore_signal(barrier, inc=1, device_id={"kin": below}, device_id_type=MESH)

    own_copy.wait()
    pl.semaphore_wait(barrier, peers - 1 + jnp.where(z < n - 1, 1, 0) + jnp.where(z > 0, 1, 0))

    def gather_copy(k):
        return pltpu.make_async_remote_copy(
            src_ref=gathered.at[0], dst_ref=gathered.at[k],
            send_sem=gather_send.at[k - 1], recv_sem=gather_recv.at[k - 1],
            device_id={"nout": peer(k)}, device_id_type=MESH,
        )

    for k in range(peers - 1, 0, -1):
        gather_copy(k).start()
    mask_copy.wait()
    keep = mask[...].astype(jnp.float32) * KEEP_SCALE
    tokens = normed_ref.shape[0]

    def drop(x, source):
        x = x.astype(jnp.float32)
        for r in range(0, tokens, 2):
            pair = [x[t : t + 1, :] * keep for t in (r, r + 1)]
            row = pl.multiple_of((source * tokens + r) * passes, 2 * passes)
            dropped[pl.ds(row, 2 * passes), :] = jnp.concatenate(pair, axis=0).astype(jnp.bfloat16)

    drop(gathered[0], mine)

    def sized(c, body):
        @pl.when(c == 0)
        def _():
            body(0, head)

        @pl.when((c > 0) & (c < chunks))
        def _():
            body(c, WIDE)

    def rise_copy(c, d, width):
        part = (c, d, slice(None), pl.ds(0, width))
        return pltpu.make_async_remote_copy(
            src_ref=rising.at[part], dst_ref=rising.at[part],
            send_sem=send_sem.at[c, d], recv_sem=rise_recv.at[c, d],
            device_id={"kin": above}, device_id_type=MESH,
        )

    def fall_copy(c, d, width):
        part = (c, d, slice(None), pl.ds(0, width))
        return pltpu.make_async_remote_copy(
            src_ref=falling.at[part], dst_ref=falling.at[part],
            send_sem=send_sem.at[c, d], recv_sem=fall_recv.at[c, d],
            device_id={"kin": below}, device_id_type=MESH,
        )

    def compute(c, width):
        slot = lax.rem(c, SLOTS)
        if not isinstance(c, int):
            @pl.when(c >= EARLY)
            def _():
                tile_copy(c, slot)(lambda copy: copy.wait())

        got = jnp.dot(dropped[...], tiles[slot, :, :width], preferred_element_type=jnp.float32)
        own[c, :, :, :width] = got.reshape(n, block, width)

        @pl.when(c + SLOTS < chunks)
        def _():
            tile_copy(c + SLOTS, slot)(lambda copy: copy.start())

    for c in range(EARLY):
        width = WIDE if c else head
        if c:
            tile_copy(c, c)(lambda copy: copy.wait())
        else:
            first_tile.wait()

        def send_early(buffer, copy_of):
            rows = dropped[pl.ds(pl.multiple_of(mine * block, block), block), :]
            part = jnp.dot(rows, tiles[c, :, :width], preferred_element_type=jnp.float32)
            buffer[c, mine, :, :width] = part.astype(jnp.bfloat16)
            copy_of(c, mine, width).start()

        @pl.when((z == 0) & (mine > 0))
        def _():
            send_early(rising, rise_copy)

        @pl.when((z == n - 1) & (mine < n - 1))
        def _():
            send_early(falling, fall_copy)

    for k in range(1, peers):
        gather_copy(k).wait_recv()
        drop(gathered[k], peer(k))

    def forward(buffer, copy_of, at_end, d):
        def body(c, width):
            sent = at_end & (d == mine) & (c < EARLY)

            @pl.when(at_end & jnp.logical_not(sent))
            def _():
                buffer[c, d, :, :width] = own[c, d, :, :width].astype(jnp.bfloat16)

            @pl.when(jnp.logical_not(at_end))
            def _():
                copy_of(c, d, width).wait_recv()
                buffer[c, d, :, :width] = (
                    buffer[c, d, :, :width].astype(jnp.float32) + own[c, d, :, :width]
                ).astype(jnp.bfloat16)

            @pl.when(jnp.logical_not(sent))
            def _():
                copy_of(c, d, width).start()
        return body

    def finish(c, width):
        @pl.when(z > 0)
        def _():
            rise_copy(c, z, width).wait_recv()
            own[c, z, :, :width] += rising[c, z, :, :width].astype(jnp.float32)

        @pl.when(z < n - 1)
        def _():
            fall_copy(c, z, width).wait_recv()
            own[c, z, :, :width] += falling[c, z, :, :width].astype(jnp.float32)

        total = own[c, z, :, :width]
        if isinstance(c, int):
            qkv_out[:, :width] = total.astype(jnp.bfloat16)
        else:
            @pl.when(c < nq)
            def _():
                col = pl.multiple_of(head + (c - 1) * WIDE, 128)
                qkv_out[:, pl.ds(col, WIDE)] = total.astype(jnp.bfloat16)

            @pl.when(c >= nq)
            def _():
                col = pl.multiple_of((c - nq) * WIDE, 128)
                up_out[:, pl.ds(col, WIDE)] = gelu(total).astype(jnp.bfloat16)

    def step(s, carry):
        sized(s, compute)

        def rise(i, carry):
            d = n - 1 - i
            sized(s - LAG * (z + i), forward(rising, rise_copy, z == 0, d))
            return carry

        def fall(d, carry):
            sized(s - LAG * (n - 1 - z + d), forward(falling, fall_copy, z == n - 1, d))
            return carry

        lax.fori_loop(0, n - 1 - z, rise, 0)
        lax.fori_loop(0, z, fall, 0)
        sized(s - LAG * (n - 1), finish)
        return carry

    lax.fori_loop(0, chunks + LAG * (n - 1), step, 0)

    for k in range(1, peers):
        gather_copy(k).wait_send()

    def drain(c, width):
        def up(i, carry):
            rise_copy(c, n - 1 - i, width).wait_send()
            return carry

        def down(i, carry):
            fall_copy(c, i, width).wait_send()
            return carry

        lax.fori_loop(0, n - 1 - z, up, 0)
        lax.fori_loop(0, z, down, 0)

    def drain_step(c, carry):
        sized(c, drain)
        return carry

    lax.fori_loop(0, chunks, drain_step, 0)


def fused(normed, keep_masks, qkv_weight, up_weight):
    n, peers = lax.axis_size("kin"), lax.axis_size("nout")
    tokens, width = normed.shape
    passes = keep_masks.shape[0]
    qkv_cols, up_cols = qkv_weight.shape[1], up_weight.shape[1]
    head = qkv_cols % WIDE or WIDE
    nq = 1 + (qkv_cols - head) // WIDE
    chunks = nq + up_cols // WIDE
    rows = tokens * peers * passes
    block = rows // n
    vmem = pl.BlockSpec(memory_space=pltpu.VMEM)
    hbm = pl.BlockSpec(memory_space=pltpu.HBM)
    qkv_out, up_out = pl.pallas_call(
        functools.partial(kernel, n, peers, passes, head, nq, chunks),
        out_shape=(
            jax.ShapeDtypeStruct((block, qkv_cols), jnp.bfloat16),
            jax.ShapeDtypeStruct((block, up_cols), jnp.bfloat16),
        ),
        in_specs=[hbm, hbm, hbm, hbm],
        out_specs=(vmem, vmem),
        scratch_shapes=[
            pltpu.VMEM((peers, tokens, width), jnp.bfloat16),
            pltpu.VMEM((passes, width), jnp.int32),
            pltpu.VMEM((rows, width), jnp.bfloat16),
            pltpu.VMEM((SLOTS, width, WIDE), jnp.bfloat16),
            pltpu.VMEM((chunks, n, block, WIDE), jnp.float32),
            pltpu.VMEM((chunks, n, block, WIDE), jnp.bfloat16),
            pltpu.VMEM((chunks, n, block, WIDE), jnp.bfloat16),
            pltpu.SemaphoreType.DMA,
            pltpu.SemaphoreType.DMA,
            pltpu.SemaphoreType.DMA((peers - 1,)),
            pltpu.SemaphoreType.DMA((peers - 1,)),
            pltpu.SemaphoreType.DMA((SLOTS,)),
            pltpu.SemaphoreType.DMA((chunks, n)),
            pltpu.SemaphoreType.DMA((chunks, n)),
            pltpu.SemaphoreType.DMA((chunks, n)),
        ],
        compiler_params=pltpu.CompilerParams(
            collective_id=0, has_side_effects=True, vmem_limit_bytes=52 * 2**20
        ),
        cost_estimate=pl.CostEstimate(
            flops=2 * rows * width * (qkv_cols + up_cols),
            bytes_accessed=2 * width * (qkv_cols + up_cols),
            transcendentals=block * up_cols,
        ),
    )(normed, keep_masks, qkv_weight, up_weight)
    own_tokens = block // passes
    return (
        qkv_out.reshape(own_tokens, passes, qkv_cols),
        up_out.reshape(own_tokens, passes, up_cols),
    )


def plain(normed, keep_masks, qkv_weight, up_weight):
    gathered = lax.all_gather(normed, "nout", axis=0, tiled=True)
    all_tokens, width = gathered.shape
    passes = keep_masks.shape[0]
    qkv_cols, up_cols = qkv_weight.shape[1], up_weight.shape[1]
    dropped = (
        gathered.astype(jnp.float32)[:, None, :]
        * keep_masks.astype(jnp.float32)[None, :, :]
        * KEEP_SCALE
    )
    rows = dropped.astype(jnp.bfloat16).reshape(all_tokens * passes, width)
    first = jnp.dot(rows, qkv_weight, preferred_element_type=jnp.float32)
    second = jnp.dot(rows, up_weight, preferred_element_type=jnp.float32)
    joined = jnp.concatenate([first, second], axis=1)
    summed = lax.psum_scatter(
        joined.reshape(all_tokens, passes, qkv_cols + up_cols).astype(jnp.bfloat16),
        "kin",
        scatter_dimension=0,
        tiled=True,
    ).astype(jnp.float32)
    qkv_out = summed[:, :, :qkv_cols].astype(jnp.bfloat16)
    hidden_out = jax.nn.gelu(summed[:, :, qkv_cols:], approximate=False).astype(jnp.bfloat16)
    return (qkv_out, hidden_out)


def local(normed, keep_masks, qkv_weight, up_weight):
    tokens, width = normed.shape
    passes = keep_masks.shape[0]
    n, peers = lax.axis_size("kin"), lax.axis_size("nout")
    aligned = (
        width % 128 == 0
        and qkv_weight.shape[1] % 128 == 0
        and up_weight.shape[1] % WIDE == 0
        and tokens % 2 == 0
        and peers & (peers - 1) == 0
        and peers == n
        and passes == 8
        and (tokens * peers * passes // n) % 16 == 0
        and (qkv_weight.shape[1] + up_weight.shape[1]) // WIDE >= SLOTS
    )
    run = fused if aligned else plain
    return run(normed, keep_masks, qkv_weight, up_weight)


def solution(mesh):
    placed = (P(("grp", "nout"), "kin"), P("grp", "kin"), P("kin", "nout"), P("kin", "nout"))
    return jax.shard_map(
        local,
        mesh=mesh,
        in_specs=placed,
        out_specs=(P(("grp", "kin"), None, "nout"), P(("grp", "kin"), None, "nout")),
        check_vma=False,
    )
```
